512 devices in a mesh: level: 8 (over x, core), row: 16 (over z), col: 4 (over y).
Axes of the slice: x: 4, y: 4, z: 16, core: 2. Of those that a mesh axis runs over, the one named last changes fastest.
Arguments:
- factor_tiles: bfloat16 [8, 64, 16, 4, 128, 128], P('level', 'row', None, 'col'), may hold values from -0.0625 to 0.0625
- tile_mask: int32 [8, 64, 16, 4], P('level', 'row', None, 'col'), may hold values from 0 to 1, as said below
- inverse_diagonal: bfloat16 [8, 16, 4, 128, 128], P('level', 'row', 'col'), may hold values from -1.5 to 1.5, as said below
- right_sides: float32 [8, 16, 4, 128, 128], P('level', 'row', 'col'), may hold values from -6 to 6
Outputs:
- forward_solution: bfloat16 [8, 16, 4, 128, 128], P('level', 'row', 'col')
- solution: bfloat16 [8, 16, 4, 128, 128], P('level', 'row', 'col')
The draws below stay inside these ranges and needn't reach their ends.
Inputs may be any that keep to these rules, and one draw needn't show every extreme that they name: `tile_mask`: 1 where the factor holds the tile, 0 where it does not; tiles are present only where |i - j| <= 32 with j = q * 4 + c, a band that follows the elimination tree. `inverse_diagonal`: each 128 x 128 block is lower triangular, the inverse of a diagonal block of the factor.
All inputs are finite; a program needn't handle non-finite values.
Results may differ from the reference program's by a relative error of at most 0.035.
Values may be sent and summed in bfloat16 or wider, within the bound.
A program may use at most 64 MiB of HBM per device.

```python
import math
import jax
import jax.numpy as jnp
from jax import lax

S = 128
R = 128
NL = 8
CLASSES = 4
NQ = 16
NSUP = 64
N_ROW = 16


def draw_inverse_diagonal(key, part):
    first, second = jax.random.split(key)
    shape = (NL, NQ, CLASSES, S, S)
    lower = jax.random.normal(first, shape, jnp.float32) * (0.5 / math.sqrt(S))
    diagonal = jax.random.uniform(second, (NL, NQ, CLASSES, S), jnp.float32, 0.5, 1.5)
    rows = lax.broadcasted_iota(jnp.int32, (S, S), 0)
    cols = lax.broadcasted_iota(jnp.int32, (S, S), 1)
    strict = (rows > cols).astype(jnp.float32)
    ident = (rows == cols).astype(jnp.float32)
    blocks = lower * strict + diagonal[..., None] * ident
    return blocks.astype(jnp.bfloat16)


def draw_tile_mask(key, part):
    first, second = jax.random.split(jax.random.fold_in(key, 7))
    share = jax.random.randint(first, (NL, NSUP, 1, 1), 1, 9)
    picks = jax.random.randint(second, (NL, NSUP, NQ, CLASSES), 0, 8)
    shape = (NL, NSUP, NQ, CLASSES)
    row_id = lax.broadcasted_iota(jnp.int32, shape, 1)
    col_id = lax.broadcasted_iota(jnp.int32, shape, 2) * CLASSES + lax.broadcasted_iota(jnp.int32, shape, 3)
    inside = jnp.abs(row_id - col_id) <= NSUP // 2
    return ((picks < share) & inside).astype(jnp.int32)


def level_of(stream_key, shape, pieces, low, largest):
    def one(axis_at, blocks):
        heights = jax.random.uniform(jax.random.fold_in(jax.random.fold_in(stream_key, 6), axis_at), (blocks,), jnp.float32, low / len(pieces), largest / len(pieces))
        return jnp.repeat(jnp.exp(heights), shape[axis_at] // blocks).reshape((-1,) + (1,) * (len(shape) - axis_at - 1))

    factor_of = one(*pieces[0])
    for cut in pieces[1:]:
        factor_of = factor_of * one(*cut)
    return factor_of


def normal_values(rng, shape, deviation, reach, pieces=(), held_as=jnp.bfloat16):
    array = jax.random.normal(rng, shape, jnp.float32) * deviation
    if len(pieces) > 0:
        array = level_of(rng, shape, pieces, -0.22, 0.18) * array
    return jnp.clip(array, min=-reach, max=reach).astype(held_as)


def setup_inputs(seed: int = 0) -> dict:
    key_of = jax.random.split(jax.random.key(seed), 5)
    factor_tiles = normal_values(key_of[0], (NL, NSUP, NQ, CLASSES, S, S), (NSUP * S) ** -0.5, 0.0625, ((0, 8), (1, 16), (3, 4)))
    tile_mask = draw_tile_mask(jax.random.fold_in(key_of[4], 71), 0)
    inverse_diagonal = draw_inverse_diagonal(jax.random.fold_in(key_of[4], 71), 0)
    right_sides = normal_values(key_of[3], (NL, NQ, CLASSES, S, R), 1.0, 6.0, ((0, 8), (1, 16), (2, 4)), jnp.float32)
    return dict(factor_tiles=factor_tiles, tile_mask=tile_mask, inverse_diagonal=inverse_diagonal, right_sides=right_sides)


def forward_sum(tiles_level, mask_level, previous):
    prev_wide = previous.astype(jnp.float32)

    def one_row(items):
        tile_row, mask_row = items
        weighted = tile_row.astype(jnp.float32) * mask_row.astype(jnp.float32)[:, :, None, None]
        weighted = weighted.reshape(NSUP, S, S)
        return jnp.einsum("jab,jbr->ar", weighted, prev_wide)

    return lax.map(one_row, (tiles_level, mask_level))


def backward_sum(tiles_level, mask_level, later):
    group_rows = NSUP // N_ROW
    tiles_grouped = tiles_level.reshape(N_ROW, group_rows, NSUP, S, S)
    mask_grouped = mask_level.reshape(N_ROW, group_rows, NSUP)
    later_grouped = later.astype(jnp.float32).reshape(N_ROW, group_rows, S, R)

    def one_group(items):
        tile_group, mask_group, values = items
        weighted = tile_group.astype(jnp.float32) * mask_group.astype(jnp.float32)[:, :, None, None]
        partial_value = jnp.einsum("ajst,asr->jtr", weighted, values)
        return partial_value.astype(jnp.bfloat16).astype(jnp.float32)

    parts = lax.map(one_group, (tiles_grouped, mask_grouped, later_grouped))
    return jnp.sum(parts, axis=0)


def reference(factor_tiles, tile_mask, inverse_diagonal, right_sides):
    sides = right_sides.reshape(NL, NSUP, S, R)
    inverse = inverse_diagonal.reshape(NL, NSUP, S, S).astype(jnp.float32)
    forward_levels = []
    previous = jnp.zeros((NSUP, S, R), jnp.bfloat16)
    for level in range(NL):
        if level > 0:
            update = forward_sum(factor_tiles[level], tile_mask[level], previous)
        else:
            update = jnp.zeros((NSUP, S, R), jnp.float32)
        values = (sides[level] - update).astype(jnp.bfloat16)
        solved = jnp.einsum("ist,itr->isr", inverse[level], values.astype(jnp.float32)).astype(jnp.bfloat16)
        forward_levels.append(solved)
        previous = solved
    backward_levels = [None] * NL
    for level in reversed(range(NL)):
        if level < NL - 1:
            update = backward_sum(factor_tiles[level + 1], tile_mask[level + 1], backward_levels[level + 1])
        else:
            update = jnp.zeros((NSUP, S, R), jnp.float32)
        values = (forward_levels[level].astype(jnp.float32) - update).astype(jnp.bfloat16)
        backward_levels[level] = jnp.einsum("its,itr->isr", inverse[level], values.astype(jnp.float32)).astype(jnp.bfloat16)
    forward_solution = jnp.stack(forward_levels).reshape(NL, NQ, CLASSES, S, R)
    solution = jnp.stack(backward_levels).reshape(NL, NQ, CLASSES, S, R)
    return forward_solution, solution
```

```python
import functools

import jax
import jax.numpy as jnp
from jax import lax
from jax.experimental import pallas as pl
from jax.experimental.pallas import tpu as pltpu
from jax.sharding import PartitionSpec as P

MESH = pl.DeviceIdType.MESH
BAND = 8
FAR_FIRST = sorted(range(-BAND, BAND + 1), key=lambda d: -abs(d))


def kernel(
    nlev, nrow, ncol, chunks,
    tiles_ref, mask_ref, inverse_ref, sides_ref,
    forward_ref, answer_ref,
    wf, wb, inv_t, sides_t,
    xin, part, part_f, yin, ysol, xsol, bin_, zout, zin, update,
    fz_send, fz_recv, fy_send, fy_recv, by_send, by_recv, bz_send, bz_recv,
):
    l, z, c = lax.axis_index("level"), lax.axis_index("row"), lax.axis_index("col")
    rows = sides_ref.shape[0] // chunks
    side = sides_ref.shape[0]
    last = nlev - 1
    others = [lax.rem(c + o, ncol) for o in range(1, ncol)]

    for q in range(nrow):
        @pl.when((q - z > BAND) | (z - q > BAND))
        def _():
            for k in range(chunks):
                xin[k, q] = jnp.zeros_like(xin[k, q])
                zin[k, q] = jnp.zeros_like(zin[k, q])

    barrier = pltpu.get_barrier_semaphore()
    for o in others:
        pl.semaphore_signal(barrier, inc=1, device_id=(l, z, o), device_id_type=MESH)

    @pl.when(l < last)
    def _():
        for q in range(nrow):
            pl.semaphore_signal(barrier, inc=1, device_id=(l + 1, q, c), device_id_type=MESH)

    @pl.when(l > 0)
    def _():
        for q in range(nrow):
            pl.semaphore_signal(barrier, inc=1, device_id=(l - 1, q, c), device_id_type=MESH)

    inv_t[...] = inverse_ref[...].T
    turned = sides_ref[...].T
    for k in range(chunks):
        sides_t[k] = turned[k * rows:(k + 1) * rows]
    update[...] = jnp.zeros_like(update)

    @pl.when(l > 0)
    def _():
        def prepare(q, carry):
            for a in range(ncol):
                present = mask_ref[a, q].astype(jnp.float32)
                tile = tiles_ref[a, q] * present.astype(jnp.bfloat16)
                wb[q, a * side:(a + 1) * side, :] = tile
                wf[q, :, a * side:(a + 1) * side] = tile.T
            return carry
        lax.fori_loop(0, nrow, prepare, 0)

    pl.semaphore_wait(
        barrier,
        (ncol - 1) + jnp.where(l > 0, nrow, 0) + jnp.where(l < last, nrow, 0),
    )

    def forward_copy(k, q):
        return pltpu.make_async_remote_copy(
            ysol.at[k], xin.at[k, z], fz_send.at[k, q], fz_recv.at[k, z],
            device_id=(l + 1, q, c), device_id_type=MESH)

    def backward_copy(k, q):
        return pltpu.make_async_remote_copy(
            zout.at[k, q], zin.at[k, z], bz_send.at[k, q], bz_recv.at[k, z],
            device_id=(l - 1, q, c), device_id_type=MESH)

    def part_copy(k, o):
        return pltpu.make_async_remote_copy(
            part.at[k, o], yin.at[k, c], fy_send.at[k, o], fy_recv.at[k, c],
            device_id=(l, z, o), device_id_type=MESH)

    def answer_copy(k, o):
        return pltpu.make_async_remote_copy(
            xsol.at[k], bin_.at[k, c], by_send.at[k, o], by_recv.at[k, c],
            device_id=(l, z, o), device_id_type=MESH)

    def arrived(dst, sem):
        pltpu.make_async_copy(dst, dst, sem).wait()

    def in_band(q):
        return (q - z <= BAND) & (z - q <= BAND)

    def forward_step(k):
        @pl.when(l > 0)
        def _():
            for q in range(nrow):
                @pl.when(in_band(q))
                def _():
                    arrived(xin.at[k, q], fz_recv.at[k, q])
            wide = jnp.concatenate([xin[k, q] for q in range(nrow)], axis=1)
            total = jnp.dot(
                wide, wf[...].reshape(nrow * side, ncol * side),
                preferred_element_type=jnp.float32)
            for a in range(ncol):
                piece = total[:, a * side:(a + 1) * side]
                part_f[a] = piece
                part[k, a] = piece.astype(jnp.bfloat16)
            for o in others:
                part_copy(k, o).start()
            for o in others:
                arrived(yin.at[k, o], fy_recv.at[k, o])
            mine = part_f[c]
            for o in others:
                mine = mine + yin[k, o].astype(jnp.float32)
            update[...] = mine

        values = (sides_t[k] - update[...]).astype(jnp.bfloat16)
        ysol[k] = jnp.dot(
            values, inv_t[...], preferred_element_type=jnp.float32).astype(jnp.bfloat16)

        @pl.when(l < last)
        def _():
            for d in FAR_FIRST:
                @pl.when((z + d >= 0) & (z + d < nrow))
                def _():
                    forward_copy(k, z + d).start()

    def backward_step(k):
        @pl.when(l < last)
        def _():
            for q in range(nrow):
                @pl.when(in_band(q))
                def _():
                    arrived(zin.at[k, q], bz_recv.at[k, q])
            update[...] = functools.reduce(
                jnp.add, [zin[k, q].astype(jnp.float32) for q in range(nrow)])

        @pl.when(l == last)
        def _():
            update[...] = jnp.zeros_like(update)

        values = (ysol[k].astype(jnp.float32) - update[...]).astype(jnp.bfloat16)
        xsol[k] = jnp.dot(
            values, inverse_ref[...], preferred_element_type=jnp.float32).astype(jnp.bfloat16)

        @pl.when(l > 0)
        def _():
            for o in others:
                answer_copy(k, o).start()
            bin_[k, c] = xsol[k]
            for o in others:
                arrived(bin_.at[k, o], by_recv.at[k, o])
            wide = jnp.concatenate([bin_[k, a] for a in range(ncol)], axis=1)
            for d in FAR_FIRST:
                @pl.when((z + d >= 0) & (z + d < nrow))
                def _():
                    zout[k, z + d] = jnp.dot(
                        wide, wb[z + d], preferred_element_type=jnp.float32
                    ).astype(jnp.bfloat16)
                    backward_copy(k, z + d).start()

    def forward_sent(k):
        @pl.when(l > 0)
        def _():
            for o in others:
                part_copy(k, o).wait_send()

        @pl.when(l < last)
        def _():
            for d in FAR_FIRST:
                @pl.when((z + d >= 0) & (z + d < nrow))
                def _():
                    forward_copy(k, z + d).wait_send()

    def backward_sent(k):
        @pl.when(l > 0)
        def _():
            for o in others:
                answer_copy(k, o).wait_send()
            for d in FAR_FIRST:
                @pl.when((z + d >= 0) & (z + d < nrow))
                def _():
                    backward_copy(k, z + d).wait_send()

    def step(t, carry):
        at_last = l == last
        is_forward = jnp.where(at_last, lax.rem(t, 2) == 0, t < chunks)
        k = jnp.where(at_last, t // 2, lax.rem(t, chunks))

        @pl.when(is_forward)
        def _():
            forward_step(k)

        @pl.when(t == chunks)
        def _():
            @pl.when(l < last)
            def _():
                lax.fori_loop(0, chunks, lambda j, x: (forward_sent(j), x)[1], 0)

        @pl.when(jnp.logical_not(is_forward))
        def _():
            backward_step(k)

        return carry

    lax.fori_loop(0, 2 * chunks, step, 0)

    @pl.when(l == last)
    def _():
        lax.fori_loop(0, chunks, lambda j, x: (forward_sent(j), x)[1], 0)

    lax.fori_loop(0, chunks, lambda j, x: (backward_sent(j), x)[1], 0)
    for k in range(chunks):
        forward_ref[k * rows:(k + 1) * rows] = ysol[k]
        answer_ref[k * rows:(k + 1) * rows] = xsol[k]


def local(factor_tiles, tile_mask, inverse_diagonal, right_sides):
    nlev, nrow, ncol = (lax.axis_size(n) for n in ("level", "row", "col"))
    tiles = factor_tiles[0, :, :, 0]
    mask = tile_mask[0, :, :, 0]
    inverse = inverse_diagonal[0, 0, 0]
    sides = right_sides[0, 0, 0]
    side, width = sides.shape
    chunks = 4
    rows = width // chunks
    bf16, f32 = jnp.bfloat16, jnp.float32
    vmem = pl.BlockSpec(memory_space=pltpu.VMEM)
    dma = pltpu.SemaphoreType.DMA
    forward, answer = pl.pallas_call(
        functools.partial(kernel, nlev, nrow, ncol, chunks),
        name="levels",
        out_shape=[jax.ShapeDtypeStruct((width, side), bf16)] * 2,
        in_specs=[vmem, pl.BlockSpec(memory_space=pltpu.SMEM), vmem, vmem],
        out_specs=[vmem, vmem],
        scratch_shapes=[
            pltpu.VMEM((nrow, side, ncol * side), bf16),
            pltpu.VMEM((nrow, ncol * side, side), bf16),
            pltpu.VMEM((side, side), bf16),
            pltpu.VMEM((chunks, rows, side), f32),
            pltpu.VMEM((chunks, nrow, rows, side), bf16),
            pltpu.VMEM((chunks, ncol, rows, side), bf16),
            pltpu.VMEM((ncol, rows, side), f32),
            pltpu.VMEM((chunks, ncol, rows, side), bf16),
            pltpu.VMEM((chunks, rows, side), bf16),
            pltpu.VMEM((chunks, rows, side), bf16),
            pltpu.VMEM((chunks, ncol, rows, side), bf16),
            pltpu.VMEM((chunks, nrow, rows, side), bf16),
            pltpu.VMEM((chunks, nrow, rows, side), bf16),
            pltpu.VMEM((rows, side), f32),
            dma((chunks, nrow)), dma((chunks, nrow)),
            dma((chunks, ncol)), dma((chunks, ncol)),
            dma((chunks, ncol)), dma((chunks, ncol)),
            dma((chunks, nrow)), dma((chunks, nrow)),
        ],
        compiler_params=pltpu.CompilerParams(
            collective_id=0, has_side_effects=True, vmem_limit_bytes=40 * 2**20),
        cost_estimate=pl.CostEstimate(flops=2**30, bytes_accessed=2**22, transcendentals=0),
    )(tiles, mask, inverse, sides)
    return (forward.T[None, None, None], answer.T[None, None, None])


def solution(mesh):
    placed = (
        P("level", "row", None, "col", None, None),
        P("level", "row", None, "col"),
        P("level", "row", "col", None, None),
        P("level", "row", "col", None, None),
    )
    return jax.shard_map(
        local,
        mesh=mesh,
        in_specs=placed,
        out_specs=(P("level", "row", "col", None, None), P("level", "row", "col", None, None)),
        check_vma=False,
    )
```

```python
import functools

import jax
import jax.numpy as jnp
from jax import lax
from jax.experimental import pallas as pl
from jax.experimental.pallas import tpu as pltpu
from jax.sharding import PartitionSpec as P

MESH = pl.DeviceIdType.MESH
BAND = 8
FAR_FIRST = sorted(range(-BAND, BAND + 1), key=lambda d: -abs(d))


def kernel(
    nlev, nrow, ncol, chunks,
    tiles_hbm, mask_hbm, inverse_hbm, sides_hbm,
    forward_ref, answer_ref,
    tiles_ref, mask_ref, inverse_ref, sides_ref,
    wf, wb, inv_t, sides_t,
    xin, part, part_f, yin, ysol, xsol, bin_, zout, zin, update,
    load_sem,
    fz_send, fz_recv, fy_send, fy_recv, by_send, by_recv, bz_send, bz_recv,
):
    l, z, c = lax.axis_index("level"), lax.axis_index("row"), lax.axis_index("col")
    rows = sides_ref.shape[0] // chunks
    side = sides_ref.shape[0]
    last = nlev - 1
    others = [lax.rem(c + o, ncol) for o in range(1, ncol)]

    loads = [
        pltpu.make_async_copy(src, dst, load_sem.at[n])
        for n, (src, dst) in enumerate((
            (sides_hbm, sides_ref), (inverse_hbm, inverse_ref),
            (mask_hbm, mask_ref), (tiles_hbm, tiles_ref)))
    ]
    for load in loads:
        load.start()

    def exists(d):
        return (z + d >= 0) & (z + d < nrow)

    for d in range(-BAND, BAND + 1):
        @pl.when(jnp.logical_not(exists(d)))
        def _():
            for k in range(chunks):
                xin[k, d + BAND] = jnp.zeros_like(xin[k, d + BAND])
                zin[k, d + BAND] = jnp.zeros_like(zin[k, d + BAND])

    barrier = pltpu.get_barrier_semaphore()
    for o in others:
        pl.semaphore_signal(barrier, inc=1, device_id=(l, z, o), device_id_type=MESH)

    @pl.when(l < last)
    def _():
        for q in range(nrow):
            pl.semaphore_signal(barrier, inc=1, device_id=(l + 1, q, c), device_id_type=MESH)

    @pl.when(l > 0)
    def _():
        for q in range(nrow):
            pl.semaphore_signal(barrier, inc=1, device_id=(l - 1, q, c), device_id_type=MESH)

    loads[0].wait()
    turned = sides_ref[...].T
    for k in range(chunks):
        sides_t[k] = turned[k * rows:(k + 1) * rows]
    loads[1].wait()
    inv_t[...] = inverse_ref[...].T
    update[...] = jnp.zeros_like(update)
    loads[2].wait()
    loads[3].wait()

    @pl.when(l > 0)
    def _():
        def prepare(slot, carry):
            q = z + slot - BAND
            at = pl.ds(pl.multiple_of(slot * side, side), side)

            @pl.when((q >= 0) & (q < nrow))
            def _():
                for a in range(ncol):
                    present = mask_ref[a, q].astype(jnp.float32)
                    tile = tiles_ref[a, q] * present.astype(jnp.bfloat16)
                    wb[slot, a * side:(a + 1) * side, :] = tile
                    wf[at, a * side:(a + 1) * side] = tile.T

            @pl.when((q < 0) | (q >= nrow))
            def _():
                wf[at, :] = jnp.zeros((side, ncol * side), wf.dtype)
            return carry
        lax.fori_loop(0, 2 * BAND + 1, prepare, 0)

    pl.semaphore_wait(
        barrier,
        (ncol - 1) + jnp.where(l > 0, nrow, 0) + jnp.where(l < last, nrow, 0),
    )

    def forward_copy(k, d):
        return pltpu.make_async_remote_copy(
            ysol.at[k], xin.at[k, BAND - d], fz_send.at[k, BAND + d], fz_recv.at[k, BAND - d],
            device_id=(l + 1, z + d, c), device_id_type=MESH)

    def backward_copy(k, d):
        return pltpu.make_async_remote_copy(
            zout.at[k, BAND + d], zin.at[k, BAND - d], bz_send.at[k, BAND + d], bz_recv.at[k, BAND - d],
            device_id=(l - 1, z + d, c), device_id_type=MESH)

    def part_copy(k, o):
        return pltpu.make_async_remote_copy(
            part.at[k, o], yin.at[k, c], fy_send.at[k, o], fy_recv.at[k, c],
            device_id=(l, z, o), device_id_type=MESH)

    def answer_copy(k, o):
        return pltpu.make_async_remote_copy(
            xsol.at[k], bin_.at[k, c], by_send.at[k, o], by_recv.at[k, c],
            device_id=(l, z, o), device_id_type=MESH)

    def arrived(dst, sem):
        pltpu.make_async_copy(dst, dst, sem).wait()

    def gather(buffer, sems, k, distances):
        for d in sorted(distances, key=abs):
            @pl.when(exists(d))
            def _():
                arrived(buffer.at[k, d + BAND], sems.at[k, d + BAND])

    near = range(-BAND + 2, BAND - 1)
    far_low, far_high = range(-BAND, -BAND + 2), range(BAND - 1, BAND + 1)
    far = [*far_low, *far_high]

    def product(k, distances):
        wide = jnp.concatenate([xin[k, d + BAND] for d in distances], axis=1)
        first = (distances[0] + BAND) * side
        return jnp.dot(
            wide, wf[first:first + len(distances) * side, :], preferred_element_type=jnp.float32)

    def forward_parts(k):
        gather(xin, fz_recv, k, near)
        total = product(k, near)
        gather(xin, fz_recv, k, far)
        total = total + (product(k, far_low) + product(k, far_high))
        for a in range(ncol):
            piece = total[:, a * side:(a + 1) * side]
            part_f[k, a] = piece
            part[k, a] = piece.astype(jnp.bfloat16)
        for o in others:
            part_copy(k, o).start()

    def forward_solve(k):
        @pl.when(l > 0)
        def _():
            mine = part_f[k, c]
            for o in others:
                arrived(yin.at[k, o], fy_recv.at[k, o])
                mine = mine + yin[k, o].astype(jnp.float32)
            update[...] = mine

        values = (sides_t[k] - update[...]).astype(jnp.bfloat16)
        ysol[k] = jnp.dot(
            values, inv_t[...], preferred_element_type=jnp.float32).astype(jnp.bfloat16)

        @pl.when(l < last)
        def _():
            for d in FAR_FIRST:
                @pl.when(exists(d))
                def _():
                    forward_copy(k, d).start()

    def backward_solve(k):
        def add(total, distances):
            return functools.reduce(
                jnp.add, [zin[k, d + BAND].astype(jnp.float32) for d in distances], total)

        @pl.when(l < last)
        def _():
            gather(zin, bz_recv, k, near)
            total = add(jnp.zeros_like(update), near)
            gather(zin, bz_recv, k, far)
            update[...] = add(total, far)

        @pl.when(l == last)
        def _():
            update[...] = jnp.zeros_like(update)

        values = (ysol[k].astype(jnp.float32) - update[...]).astype(jnp.bfloat16)
        xsol[k] = jnp.dot(
            values, inverse_ref[...], preferred_element_type=jnp.float32).astype(jnp.bfloat16)

        @pl.when(l > 0)
        def _():
            for o in others:
                answer_copy(k, o).start()
            bin_[k, c] = xsol[k]

    def backward_parts(k):
        for o in others:
            arrived(bin_.at[k, o], by_recv.at[k, o])
        wide = jnp.concatenate([bin_[k, a] for a in range(ncol)], axis=1)
        for d in FAR_FIRST:
            @pl.when(exists(d))
            def _():
                zout[k, d + BAND] = jnp.dot(
                    wide, wb[d + BAND], preferred_element_type=jnp.float32
                ).astype(jnp.bfloat16)
                backward_copy(k, d).start()

    def forward_sent(k):
        @pl.when(l > 0)
        def _():
            for o in others:
                part_copy(k, o).wait_send()

        @pl.when(l < last)
        def _():
            for d in FAR_FIRST:
                @pl.when(exists(d))
                def _():
                    forward_copy(k, d).wait_send()

    def backward_sent(k):
        @pl.when(l > 0)
        def _():
            for o in others:
                answer_copy(k, o).wait_send()
            for d in FAR_FIRST:
                @pl.when(exists(d))
                def _():
                    backward_copy(k, d).wait_send()

    at_last = l == last
    turn = jnp.where(at_last, 1, chunks + 1)

    def step(t, carry):
        def stage(k, wanted, work):
            @pl.when((k >= 0) & (k < chunks) & wanted)
            def _():
                work(k)

        stage(t, l > 0, forward_parts)
        stage(t - 1, True, forward_solve)
        stage(t - turn, True, backward_solve)
        stage(t - turn - 1, l > 0, backward_parts)
        stage(t - chunks - 1, True, forward_sent)
        return carry

    lax.fori_loop(0, 2 * chunks + 2, step, 0)
    lax.fori_loop(0, chunks, lambda j, x: (backward_sent(j), x)[1], 0)
    for k in range(chunks):
        forward_ref[k * rows:(k + 1) * rows] = ysol[k]
        answer_ref[k * rows:(k + 1) * rows] = xsol[k]


def local(factor_tiles, tile_mask, inverse_diagonal, right_sides):
    nlev, nrow, ncol = (lax.axis_size(n) for n in ("level", "row", "col"))
    tiles = factor_tiles[0, :, :, 0]
    mask = tile_mask[0, :, :, 0]
    inverse = inverse_diagonal[0, 0, 0]
    sides = right_sides[0, 0, 0]
    side, width = sides.shape
    chunks = 4
    rows = width // chunks
    bf16, f32 = jnp.bfloat16, jnp.float32
    vmem = pl.BlockSpec(memory_space=pltpu.VMEM)
    hbm = pl.BlockSpec(memory_space=pltpu.HBM)
    dma = pltpu.SemaphoreType.DMA
    slots = 2 * BAND + 1
    forward, answer = pl.pallas_call(
        functools.partial(kernel, nlev, nrow, ncol, chunks),
        name="levels",
        out_shape=[jax.ShapeDtypeStruct((width, side), bf16)] * 2,
        in_specs=[hbm] * 4,
        out_specs=[vmem, vmem],
        scratch_shapes=[
            pltpu.VMEM(tiles.shape, bf16),
            pltpu.SMEM(mask.shape, mask.dtype),
            pltpu.VMEM(inverse.shape, bf16),
            pltpu.VMEM(sides.shape, f32),
            pltpu.VMEM((slots * side, ncol * side), bf16),
            pltpu.VMEM((slots, ncol * side, side), bf16),
            pltpu.VMEM((side, side), bf16),
            pltpu.VMEM((chunks, rows, side), f32),
            pltpu.VMEM((chunks, slots, rows, side), bf16),
            pltpu.VMEM((chunks, ncol, rows, side), bf16),
            pltpu.VMEM((chunks, ncol, rows, side), f32),
            pltpu.VMEM((chunks, ncol, rows, side), bf16),
            pltpu.VMEM((chunks, rows, side), bf16),
            pltpu.VMEM((chunks, rows, side), bf16),
            pltpu.VMEM((chunks, ncol, rows, side), bf16),
            pltpu.VMEM((chunks, slots, rows, side), bf16),
            pltpu.VMEM((chunks, slots, rows, side), bf16),
            pltpu.VMEM((rows, side), f32),
            dma((4,)),
            dma((chunks, slots)), dma((chunks, slots)),
            dma((chunks, ncol)), dma((chunks, ncol)),
            dma((chunks, ncol)), dma((chunks, ncol)),
            dma((chunks, slots)), dma((chunks, slots)),
        ],
        compiler_params=pltpu.CompilerParams(
            collective_id=0, has_side_effects=True, vmem_limit_bytes=60 * 2**20),
        cost_estimate=pl.CostEstimate(flops=2**30, bytes_accessed=2**22, transcendentals=0),
    )(tiles, mask, inverse, sides)
    return (forward.T[None, None, None], answer.T[None, None, None])


def solution(mesh):
    placed = (
        P("level", "row", None, "col", None, None),
        P("level", "row", None, "col"),
        P("level", "row", "col", None, None),
        P("level", "row", "col", None, None),
    )
    return jax.shard_map(
        local,
        mesh=mesh,
        in_specs=placed,
        out_specs=(P("level", "row", "col", None, None), P("level", "row", "col", None, None)),
        check_vma=False,
    )
```

```python
import functools

import jax
import jax.numpy as jnp
from jax import lax
from jax.experimental import pallas as pl
from jax.experimental.pallas import tpu as pltpu
from jax.sharding import PartitionSpec as P

MESH = pl.DeviceIdType.MESH
BAND = 8
SLOTS = 2 * BAND + 1
HALF = BAND + 1


def kernel(
    nlev, nrow, ncol, chunks, whole_from, early_from,
    tiles_hbm, mask_hbm, inverse_hbm, sides_hbm,
    forward_ref, answer_ref,
    tiles_ref, mask_ref, inverse_ref, sides_ref,
    wf, wb, inv, inv_t, sides_row, sides_use,
    xin, part, part_f, yin, ysol, zout, zin, update,
    ystage, ysplit, yblock, yturned, xstage, xblock, xturned,
    load_sem, fz_send, fz_recv, fy_send, fy_recv, bz_send, bz_recv,
    bulk_send, bulk_recv, d_send, d_recv, s_send, s_recv, y_send, y_recv, x_send, x_recv,
):
    l, z, c = lax.axis_index("level"), lax.axis_index("row"), lax.axis_index("col")
    side, width = sides_ref.shape
    rows = width // chunks
    unit = rows // ncol
    last = nlev - 1
    bf16, f32 = jnp.bfloat16, jnp.float32
    others = [lax.rem(c + o, ncol) for o in range(1, ncol)]
    after, before = others[0], others[-1]
    split_from = whole_from - 1

    loads = [
        pltpu.make_async_copy(src, dst, load_sem.at[n])
        for n, (src, dst) in enumerate((
            (sides_hbm, sides_ref), (inverse_hbm, inverse_ref),
            (mask_hbm, mask_ref), (tiles_hbm, tiles_ref)))
    ]
    for load in loads:
        load.start()

    def exists(d):
        return (z + d >= 0) & (z + d < nrow)

    for d in range(-BAND, BAND + 1):
        @pl.when(jnp.logical_not(exists(d)))
        def _():
            for k in range(chunks):
                xin[k, d + BAND] = jnp.zeros_like(xin[k, d + BAND])
                zin[k, d + BAND] = jnp.zeros_like(zin[k, d + BAND])

    barrier = pltpu.get_barrier_semaphore()
    for o in others:
        pl.semaphore_signal(barrier, inc=1, device_id=(l, z, o), device_id_type=MESH)

    @pl.when(l < last)
    def _():
        for q in range(nrow):
            pl.semaphore_signal(barrier, inc=1, device_id=(l + 1, q, c), device_id_type=MESH)

    @pl.when(l > 0)
    def _():
        for q in range(nrow):
            pl.semaphore_signal(barrier, inc=1, device_id=(l - 1, q, c), device_id_type=MESH)

    loads[0].wait()
    turned = sides_ref[...].T
    for o in range(ncol):
        sides_row[o] = turned[o * rows:(o + 1) * rows]
    loads[1].wait()
    inv[c] = inverse_ref[...]
    inv_t[c] = inverse_ref[...].T
    update[...] = jnp.zeros_like(update)
    loads[2].wait()
    loads[3].wait()

    @pl.when(l > 0)
    def _():
        def prepare(slot, carry):
            q = z + slot - BAND

            @pl.when((q >= 0) & (q < nrow))
            def _():
                for a in range(ncol):
                    present = mask_ref[a, q].astype(f32)
                    tile = tiles_ref[a, q] * present.astype(bf16)
                    wb[slot, c, a * side:(a + 1) * side, :] = tile
                    wf[slot, :, a * side:(a + 1) * side] = tile.T

            @pl.when((q < 0) | (q >= nrow))
            def _():
                wb[slot, c] = jnp.zeros((ncol * side, side), bf16)
                wf[slot] = jnp.zeros((side, ncol * side), bf16)
            return carry
        lax.fori_loop(0, SLOTS, prepare, 0)

    pl.semaphore_wait(
        barrier,
        (ncol - 1) + jnp.where(l > 0, nrow, 0) + jnp.where(l < last, nrow, 0),
    )

    def remote(src, dst, send, recv, device):
        return pltpu.make_async_remote_copy(
            src, dst, send, recv, device_id=device, device_id_type=MESH)

    def arrived(dst, sem):
        pltpu.make_async_copy(dst, dst, sem).wait()

    def forward_copy(k, d):
        return remote(
            ysol.at[k], xin.at[k, BAND - d], fz_send.at[k, BAND + d], fz_recv.at[k, BAND - d],
            (l + 1, z + d, c))

    def backward_copy(k, d):
        return remote(
            zout.at[k, BAND + d], zin.at[k, BAND - d], bz_send.at[k, BAND + d],
            bz_recv.at[k, BAND - d], (l - 1, z + d, c))

    def part_copy(k, o):
        return remote(
            part.at[k, o], yin.at[k, c], fy_send.at[k, o], fy_recv.at[k, c], (l, z, o))

    def turn_copy(src, dst, send, recv, o):
        return remote(src.at[o], dst.at[c], send.at[o], recv.at[c], (l, z, o))

    def turn_start(src, dst, send, recv):
        for o in others:
            turn_copy(src, dst, send, recv, o).start()
        dst[c] = src[c]

    def turn_arrived(dst, recv):
        for o in others:
            arrived(dst.at[o], recv.at[o])

    def turn_sent(src, dst, send, recv):
        for o in others:
            turn_copy(src, dst, send, recv, o).wait_send()

    def inverse_copy(o):
        return remote(inv.at[c], inv.at[c], d_send.at[o], d_recv.at[c], (l, z, o))

    low, high = pl.ds(0, HALF), pl.ds(HALF, SLOTS - HALF)

    def bulk_copy(slots, owner, n, device):
        return remote(
            wb.at[slots, owner], wb.at[slots, owner], bulk_send.at[n], bulk_recv.at[n],
            (l, z, device))

    def bulk_own():
        return [
            bulk_copy(low, c, 0, after), bulk_copy(high, c, 3, before),
            bulk_copy(high, c, 1, after), bulk_copy(low, c, 2, before),
        ]

    def bulk_passed():
        return [bulk_copy(low, before, 4, after), bulk_copy(high, after, 5, before)]

    def spread_tiles():
        for copy in bulk_own():
            copy.start()
        to_after, to_before = bulk_passed()
        arrived(wb.at[low, before], bulk_recv.at[0])
        to_after.start()
        arrived(wb.at[high, after], bulk_recv.at[3])
        to_before.start()
        arrived(wb.at[high, before], bulk_recv.at[1])
        arrived(wb.at[low, after], bulk_recv.at[2])
        opposite = others[1]
        arrived(wb.at[low, opposite], bulk_recv.at[4])
        arrived(wb.at[high, opposite], bulk_recv.at[5])

    def await_slot(buffer, sems, k, d):
        @pl.when(exists(d))
        def _():
            arrived(buffer.at[k, d + BAND], sems.at[k, d + BAND])

    def stacked(block, k):
        at = pl.ds(pl.multiple_of(k * unit, unit), unit)
        return jnp.concatenate([block[o, at] for o in range(ncol)], axis=0)

    def put(block, k, values):
        at = pl.ds(pl.multiple_of(k * unit, unit), unit)
        for o in range(ncol):
            block[o, at] = values[o * unit:(o + 1) * unit]

    def to_lanes(values):
        return jnp.concatenate([values[o * unit:(o + 1) * unit] for o in range(ncol)], axis=1)

    def to_rows(values):
        return jnp.concatenate([values[:, o * side:(o + 1) * side] for o in range(ncol)], axis=0)

    def tiles_of(slot):
        return jnp.concatenate([wb[slot, o] for o in range(ncol)], axis=1)

    def send_forward(k):
        @pl.when(l < last)
        def _():
            def at_distance(n, carry):
                for d in (n - BAND, BAND - n):
                    @pl.when(exists(d))
                    def _():
                        forward_copy(k, d).start()
                return carry
            lax.fori_loop(0, BAND, at_distance, 0)
            forward_copy(k, 0).start()

    def forward_parts(k):
        def at_distance(n, total):
            await_slot(xin, fz_recv, k, -n)
            await_slot(xin, fz_recv, k, n)
            wide = jnp.concatenate([xin[k, BAND - n], xin[k, BAND + n]], axis=1)
            weights = jnp.concatenate([wf[BAND - n], wf[BAND + n]], axis=0)
            return total + jnp.dot(wide, weights, preferred_element_type=f32)

        await_slot(xin, fz_recv, k, 0)
        total = lax.fori_loop(
            1, BAND + 1, at_distance,
            jnp.dot(xin[k, BAND], wf[BAND], preferred_element_type=f32))

        @pl.when(l < split_from)
        def _():
            for o in range(ncol):
                part_f[k, o] = total[:, o * side:(o + 1) * side]

        @pl.when(l == split_from)
        def _():
            for o in range(ncol):
                part_f[k, o] = to_rows(total[o * unit:(o + 1) * unit])

        for o in range(ncol):
            part[k, o] = part_f[k, o].astype(bf16)
        for o in others:
            part_copy(k, o).start()

    def add_parts(k):
        mine = part_f[k, c]
        for o in others:
            arrived(yin.at[k, o], fy_recv.at[k, o])
            mine = mine + yin[k, o].astype(f32)
        update[...] = mine

    def forward_row(k):
        @pl.when(l > 0)
        def _():
            add_parts(k)

        values = (stacked(sides_use, k) - update[...]).astype(bf16)
        solved = jnp.dot(values, inv_t[c], preferred_element_type=f32).astype(bf16)
        ysol[k] = solved
        send_forward(k)
        put(ystage, k, solved.astype(f32))

    def forward_split(k):
        @pl.when(l == split_from)
        def _():
            add_parts(k)

        @pl.when(l > split_from)
        def _():
            def product(slot):
                wide = to_lanes(xin[k, slot].astype(f32)).astype(bf16)
                return lax.dot_general(
                    wide, tiles_of(slot), (((1,), (1,)), ((), ())), preferred_element_type=f32)

            def at_distance(n, total):
                await_slot(xin, fz_recv, k, -n)
                await_slot(xin, fz_recv, k, n)
                return total + (product(BAND - n) + product(BAND + n))

            await_slot(xin, fz_recv, k, 0)
            total = lax.fori_loop(1, BAND + 1, at_distance, product(BAND))
            update[...] = to_rows(total)

        values = stacked(sides_use, k) - update[...]
        solved = jnp.concatenate(
            [
                jnp.dot(values[o * unit:(o + 1) * unit].astype(bf16), inv_t[o],
                        preferred_element_type=f32)
                for o in range(ncol)
            ],
            axis=0,
        ).astype(bf16)
        ysol[k] = solved
        send_forward(k)
        put(ystage, k, solved.astype(f32))
        put(ysplit, k, solved.astype(f32))

    def backward_step(k):
        def add(total, distances):
            return functools.reduce(
                jnp.add, [zin[k, d + BAND].astype(f32) for d in distances], total)

        @pl.when(l < last)
        def _():
            near = sorted(range(-BAND + 1, BAND), key=abs)
            for d in near:
                await_slot(zin, bz_recv, k, d)
            total = add(jnp.zeros_like(update), near)
            await_slot(zin, bz_recv, k, -BAND)
            await_slot(zin, bz_recv, k, BAND)
            update[...] = add(total, (-BAND, BAND))

        @pl.when(l == last)
        def _():
            update[...] = jnp.zeros_like(update)

        values = stacked(ysplit, k) - update[...]
        wide = jnp.concatenate(
            [
                jnp.dot(values[o * unit:(o + 1) * unit].astype(bf16), inv[o],
                        preferred_element_type=f32)
                for o in range(ncol)
            ],
            axis=1,
        ).astype(bf16)

        @pl.when(l > 0)
        def _():
            def send(d):
                @pl.when(exists(d))
                def _():
                    zout[k, d + BAND] = to_rows(jnp.dot(
                        wide, tiles_of(d + BAND), preferred_element_type=f32)).astype(bf16)
                    backward_copy(k, d).start()

            def at_distance(n, carry):
                send(n - BAND)
                send(BAND - n)
                return carry
            lax.fori_loop(0, BAND, at_distance, 0)
            send(0)

        put(xstage, k, to_rows(wide.astype(f32)))

    def sent(copy_of):
        def one(k, carry):
            for d in range(-BAND, BAND + 1):
                @pl.when(exists(d))
                def _():
                    copy_of(k, d).wait_send()
            return carry
        lax.fori_loop(0, chunks, one, 0)

    def middle():
        yblock[...] = ystage[...].astype(bf16)
        turn_start(yblock, yturned, y_send, y_recv)

        @pl.when((l > 0) & (l < early_from))
        def _():
            spread_tiles()

        @pl.when(l < last)
        def _():
            sent(forward_copy)

        @pl.when((l > 0) & (l < whole_from))
        def _():
            def one(k, carry):
                for o in others:
                    part_copy(k, o).wait_send()
                return carry
            lax.fori_loop(0, chunks, one, 0)

        turn_arrived(yturned, y_recv)
        turn_sent(yblock, yturned, y_send, y_recv)

        @pl.when(l < split_from)
        def _():
            ysplit[...] = yturned[...].astype(f32)
            forward_ref[...] = yblock[...].reshape(width, side)

        @pl.when(l >= split_from)
        def _():
            forward_ref[...] = yturned[...].reshape(width, side)

    for o in others:
        inverse_copy(o).start()

    @pl.when(l < split_from)
    def _():
        sides_use[...] = sides_row[...]

    @pl.when(l >= split_from)
    def _():
        turn_start(sides_row, sides_use, s_send, s_recv)
        turn_arrived(sides_use, s_recv)
        for o in others:
            arrived(inv.at[o], d_recv.at[o])
            inv_t[o] = inv[o].T
        turn_sent(sides_row, sides_use, s_send, s_recv)

    @pl.when(l >= early_from)
    def _():
        spread_tiles()

    at_last = l == last
    turn = jnp.where(at_last, 1, chunks + 1)

    def step(t, carry):
        def stage(k, wanted, work):
            @pl.when((k >= 0) & (k < chunks) & wanted)
            def _():
                work(k)

        stage(t, (l > 0) & (l < whole_from), forward_parts)
        stage(t - 1, l < split_from, forward_row)
        stage(t - 1, l >= split_from, forward_split)
        stage(t - turn, True, backward_step)

        @pl.when(t == chunks)
        def _():
            @pl.when(l < split_from)
            def _():
                for o in others:
                    arrived(inv.at[o], d_recv.at[o])
            middle()
        return carry

    lax.fori_loop(0, 2 * chunks + 1, step, 0)

    xblock[...] = xstage[...].astype(bf16)
    turn_start(xblock, xturned, x_send, x_recv)
    for o in others:
        inverse_copy(o).wait_send()

    @pl.when(l > 0)
    def _():
        sent(backward_copy)
        for copy in (*bulk_own(), *bulk_passed()):
            copy.wait_send()
    turn_arrived(xturned, x_recv)
    answer_ref[...] = xturned[...].reshape(width, side)
    turn_sent(xblock, xturned, x_send, x_recv)


def local(factor_tiles, tile_mask, inverse_diagonal, right_sides):
    nlev, nrow, ncol = (lax.axis_size(n) for n in ("level", "row", "col"))
    tiles = factor_tiles[0, :, :, 0]
    mask = tile_mask[0, :, :, 0]
    inverse = inverse_diagonal[0, 0, 0]
    sides = right_sides[0, 0, 0]
    side, width = sides.shape
    chunks = 4
    rows = width // chunks
    bf16, f32 = jnp.bfloat16, jnp.float32
    vmem = pl.BlockSpec(memory_space=pltpu.VMEM)
    hbm = pl.BlockSpec(memory_space=pltpu.HBM)
    dma = pltpu.SemaphoreType.DMA
    blocks = (ncol, rows, side)
    forward, answer = pl.pallas_call(
        functools.partial(kernel, nlev, nrow, ncol, chunks, nlev - 3, nlev - 3),
        name="levels",
        out_shape=[jax.ShapeDtypeStruct((width, side), bf16)] * 2,
        in_specs=[hbm] * 4,
        out_specs=[vmem, vmem],
        scratch_shapes=[
            pltpu.VMEM(tiles.shape, bf16),
            pltpu.SMEM(mask.shape, mask.dtype),
            pltpu.VMEM(inverse.shape, bf16),
            pltpu.VMEM(sides.shape, f32),
            pltpu.VMEM((SLOTS, side, ncol * side), bf16),
            pltpu.VMEM((SLOTS, ncol, ncol * side, side), bf16),
            pltpu.VMEM((ncol, side, side), bf16),
            pltpu.VMEM((ncol, side, side), bf16),
            pltpu.VMEM(blocks, f32),
            pltpu.VMEM(blocks, f32),
            pltpu.VMEM((chunks, SLOTS, rows, side), bf16),
            pltpu.VMEM((chunks, *blocks), bf16),
            pltpu.VMEM((chunks, *blocks), f32),
            pltpu.VMEM((chunks, *blocks), bf16),
            pltpu.VMEM((chunks, rows, side), bf16),
            pltpu.VMEM((chunks, SLOTS, rows, side), bf16),
            pltpu.VMEM((chunks, SLOTS, rows, side), bf16),
            pltpu.VMEM((rows, side), f32),
            pltpu.VMEM(blocks, f32),
            pltpu.VMEM(blocks, f32),
            pltpu.VMEM(blocks, bf16),
            pltpu.VMEM(blocks, bf16),
            pltpu.VMEM(blocks, f32),
            pltpu.VMEM(blocks, bf16),
            pltpu.VMEM(blocks, bf16),
            dma((4,)),
            dma((chunks, SLOTS)), dma((chunks, SLOTS)),
            dma((chunks, ncol)), dma((chunks, ncol)),
            dma((chunks, SLOTS)), dma((chunks, SLOTS)),
            dma((6,)), dma((6,)),
            *[dma((ncol,)) for _ in range(8)],
        ],
        compiler_params=pltpu.CompilerParams(
            collective_id=0, has_side_effects=True, vmem_limit_bytes=60 * 2**20),
        cost_estimate=pl.CostEstimate(flops=2**30, bytes_accessed=2**22, transcendentals=0),
    )(tiles, mask, inverse, sides)
    return (forward.T[None, None, None], answer.T[None, None, None])


def solution(mesh):
    placed = (
        P("level", "row", None, "col", None, None),
        P("level", "row", None, "col"),
        P("level", "row", "col", None, None),
        P("level", "row", "col", None, None),
    )
    return jax.shard_map(
        local,
        mesh=mesh,
        in_specs=placed,
        out_specs=(P("level", "row", "col", None, None), P("level", "row", "col", None, None)),
        check_vma=False,
    )
```

```python
import functools

import jax
import jax.numpy as jnp
from jax import lax
from jax.experimental import pallas as pl
from jax.experimental.pallas import tpu as pltpu
from jax.sharding import PartitionSpec as P

MESH = pl.DeviceIdType.MESH
BAND = 8
SLOTS = 2 * BAND + 1
HALF = BAND + 1
FAR_FIRST = sorted(range(-BAND, BAND + 1), key=lambda d: -abs(d))


def kernel(
    nlev, nrow, ncol, chunks, whole_from,
    tiles_hbm, mask_hbm, inverse_hbm, sides_hbm,
    forward_ref, answer_ref,
    tiles_ref, mask_ref, inverse_ref, sides_ref,
    wt, wb, inv, inv_t, sides_row, sides_use,
    xin, part, part_f, yin, ysol, zout, zin, update,
    ystage, ysplit, yblock, yturned, xstage, xblock, xturned,
    load_sem, fz_send, fz_recv, fy_send, fy_recv, bz_send, bz_recv,
    bulk_send, bulk_recv, d_send, d_recv, s_send, s_recv, y_send, y_recv, x_send, x_recv,
    sides_guest, inv_guest, inv_t_guest, ysplit_guest, xstage_guest, yblock_guest, xblock_guest,
    ship_send, ship_recv, go_sem,
):
    l, z, c = lax.axis_index("level"), lax.axis_index("row"), lax.axis_index("col")
    side, width = sides_ref.shape
    rows = width // chunks
    unit = rows // ncol
    last = nlev - 1
    bf16, f32 = jnp.bfloat16, jnp.float32
    others = [lax.rem(c + o, ncol) for o in range(1, ncol)]
    after, before = others[0], others[-1]
    split_from = whole_from - 1
    up, down = lax.rem(l + 1, last), lax.rem(l + last - 1, last)

    loads = [
        pltpu.make_async_copy(src, dst, load_sem.at[n])
        for n, (src, dst) in enumerate((
            (sides_hbm, sides_ref), (inverse_hbm, inverse_ref),
            (mask_hbm, mask_ref), (tiles_hbm, tiles_ref)))
    ]
    for load in loads:
        load.start()

    def exists(d):
        return (z + d >= 0) & (z + d < nrow)

    for d in range(-BAND, BAND + 1):
        @pl.when(jnp.logical_not(exists(d)))
        def _():
            for k in range(chunks):
                xin[k, d + BAND] = jnp.zeros_like(xin[k, d + BAND])
                zin[k, d + BAND] = jnp.zeros_like(zin[k, d + BAND])

    barrier = pltpu.get_barrier_semaphore()
    for o in others:
        pl.semaphore_signal(barrier, inc=1, device_id=(l, z, o), device_id_type=MESH)

    @pl.when(l < last)
    def _():
        for q in range(nrow):
            pl.semaphore_signal(barrier, inc=1, device_id=(up, q, c), device_id_type=MESH)
            pl.semaphore_signal(barrier, inc=1, device_id=(down, q, c), device_id_type=MESH)

    @pl.when(l == 0)
    def _():
        pl.semaphore_signal(barrier, inc=1, device_id=(last, z, c), device_id_type=MESH)

    @pl.when(l == last)
    def _():
        pl.semaphore_signal(barrier, inc=1, device_id=(0, z, c), device_id_type=MESH)

    loads[0].wait()
    turned = sides_ref[...].T
    for o in range(ncol):
        sides_row[o] = turned[o * rows:(o + 1) * rows]
    loads[1].wait()
    inv[c] = inverse_ref[...]
    inv_t[c] = inverse_ref[...].T
    update[...] = jnp.zeros_like(update)
    loads[2].wait()
    loads[3].wait()

    @pl.when(l > 0)
    def _():
        def prepare(slot, carry):
            q = z + slot - BAND

            @pl.when((q >= 0) & (q < nrow))
            def _():
                for a in range(ncol):
                    present = mask_ref[a, q].astype(f32)
                    tile = tiles_ref[a, q] * present.astype(bf16)
                    wb[slot, c, a * side:(a + 1) * side, :] = tile
                    wt[slot, c, :, a * side:(a + 1) * side] = tile.T

            @pl.when((q < 0) | (q >= nrow))
            def _():
                wb[slot, c] = jnp.zeros((ncol * side, side), bf16)
                wt[slot, c] = jnp.zeros((side, ncol * side), bf16)
            return carry
        lax.fori_loop(0, SLOTS, prepare, 0)

    pl.semaphore_wait(
        barrier,
        (ncol - 1)
        + jnp.where(l < last, 2 * nrow, 1)
        + jnp.where(l == 0, 1, 0),
    )

    def remote(src, dst, send, recv, device):
        return pltpu.make_async_remote_copy(
            src, dst, send, recv, device_id=device, device_id_type=MESH)

    def arrived(dst, sem):
        pltpu.make_async_copy(dst, dst, sem).wait()

    def forward_copy(k, d):
        return remote(
            ysol.at[k], xin.at[k, BAND - d], fz_send.at[k, BAND + d], fz_recv.at[k, BAND - d],
            (up, z + d, c))

    def backward_copy(k, d):
        return remote(
            zout.at[k, BAND + d], zin.at[k, BAND - d], bz_send.at[k, BAND + d],
            bz_recv.at[k, BAND - d], (down, z + d, c))

    def part_copy(k, o):
        return remote(
            part.at[k, o], yin.at[k, c], fy_send.at[k, o], fy_recv.at[k, c], (l, z, o))

    def turn_copy(src, dst, send, recv, o):
        return remote(src.at[o], dst.at[c], send.at[o], recv.at[c], (l, z, o))

    def turn_start(src, dst, send, recv):
        for o in others:
            turn_copy(src, dst, send, recv, o).start()
        dst[c] = src[c]

    def turn_arrived(dst, recv):
        for o in others:
            arrived(dst.at[o], recv.at[o])

    def turn_sent(src, dst, send, recv):
        for o in others:
            turn_copy(src, dst, send, recv, o).wait_send()

    def inverse_copy(o):
        return remote(inv.at[c], inv.at[c], d_send.at[o], d_recv.at[c], (l, z, o))

    low, high = pl.ds(0, HALF), pl.ds(HALF, SLOTS - HALF)

    def bulk_copy(slots, owner, n, device):
        return remote(
            wb.at[slots, owner], wb.at[slots, owner], bulk_send.at[n], bulk_recv.at[n],
            (l, z, device))

    def bulk_own():
        return [
            bulk_copy(low, c, 0, after), bulk_copy(high, c, 3, before),
            bulk_copy(high, c, 1, after), bulk_copy(low, c, 2, before),
        ]

    def bulk_passed():
        return [bulk_copy(low, before, 4, after), bulk_copy(high, after, 5, before)]

    opposite = others[1]

    def transpose_tiles(owner):
        @pl.when((l >= whole_from) | (l == 0))
        def _():
            def one(slot, carry):
                for a in range(ncol):
                    at = slice(a * side, (a + 1) * side)
                    wt[slot, owner, :, at] = wb[slot, owner, at, :].T
                return carry
            lax.fori_loop(0, SLOTS, one, 0)

    def spread_start():
        for copy in bulk_own():
            copy.start()

    def spread_pass_on():
        to_after, to_before = bulk_passed()
        arrived(wb.at[low, before], bulk_recv.at[0])
        to_after.start()
        arrived(wb.at[high, after], bulk_recv.at[3])
        to_before.start()
        arrived(wb.at[high, before], bulk_recv.at[1])
        arrived(wb.at[low, after], bulk_recv.at[2])

    def spread_end():
        transpose_tiles(before)
        transpose_tiles(after)
        arrived(wb.at[low, opposite], bulk_recv.at[4])
        arrived(wb.at[high, opposite], bulk_recv.at[5])
        transpose_tiles(opposite)

    def ship(n, src, dst, device):
        return remote(src, dst, ship_send.at[n], ship_recv.at[n], (device, z, c))

    def ship_out():
        return [
            ship(1, sides_use, sides_guest, 0), ship(2, inv, inv_guest, 0),
            ship(3, inv_t, inv_t_guest, 0),
            ship(0, wb.at[:, c], wb.at[:, c], 0),
        ]

    def ship_back_y():
        return ship(4, yblock_guest, yblock, last)

    def ship_back_x():
        return ship(5, xblock_guest, xblock, last)

    def go(device):
        pl.semaphore_signal(go_sem, inc=1, device_id=(device, z, c), device_id_type=MESH)

    def await_slot(buffer, sems, k, d):
        @pl.when(exists(d))
        def _():
            arrived(buffer.at[k, d + BAND], sems.at[k, d + BAND])

    def stacked(block, k):
        at = pl.ds(pl.multiple_of(k * unit, unit), unit)
        return jnp.concatenate([block[o, at] for o in range(ncol)], axis=0)

    def put(block, k, values):
        at = pl.ds(pl.multiple_of(k * unit, unit), unit)
        for o in range(ncol):
            block[o, at] = values[o * unit:(o + 1) * unit]

    def to_lanes(values):
        return jnp.concatenate([values[o * unit:(o + 1) * unit] for o in range(ncol)], axis=1)

    def to_rows(values):
        return jnp.concatenate([values[:, o * side:(o + 1) * side] for o in range(ncol)], axis=0)

    def tiles_of(slot):
        return jnp.concatenate([wb[slot, o] for o in range(ncol)], axis=1)

    def send_forward(k):
        for d in FAR_FIRST:
            @pl.when(exists(d))
            def _():
                forward_copy(k, d).start()

    near = range(-BAND + 3, BAND - 2)
    middling = [-BAND + 2, BAND - 2, -BAND + 1, BAND - 1]
    far = [-BAND, BAND]

    def await_slots(buffer, sems, k, distances):
        for d in sorted(distances, key=abs):
            await_slot(buffer, sems, k, d)

    def forward_parts(k):
        def product(distances):
            wide = jnp.concatenate([xin[k, d + BAND] for d in distances], axis=1)
            weights = jnp.concatenate([wt[d + BAND, c] for d in distances], axis=0)
            return jnp.dot(wide, weights, preferred_element_type=f32)

        total = 0.0
        for distances in (near, middling, far):
            await_slots(xin, fz_recv, k, distances)
            total = total + product(distances)

        @pl.when(l < split_from)
        def _():
            for o in range(ncol):
                part_f[k, o] = total[:, o * side:(o + 1) * side]

        @pl.when(l == split_from)
        def _():
            for o in range(ncol):
                part_f[k, o] = to_rows(total[o * unit:(o + 1) * unit])

        for o in range(ncol):
            part[k, o] = part_f[k, o].astype(bf16)
        for o in others:
            part_copy(k, o).start()

    def add_parts(k):
        mine = part_f[k, c]
        for o in others:
            arrived(yin.at[k, o], fy_recv.at[k, o])
            mine = mine + yin[k, o].astype(f32)
        update[...] = mine

    def forward_row(k):
        @pl.when(l > 0)
        def _():
            add_parts(k)

        values = (stacked(sides_use, k) - update[...]).astype(bf16)
        solved = jnp.dot(values, inv_t[c], preferred_element_type=f32).astype(bf16)
        ysol[k] = solved
        send_forward(k)
        put(ystage, k, solved.astype(f32))

    def whole_product(k):
        def product(distances):
            return functools.reduce(jnp.add, [
                jnp.dot(
                    to_lanes(xin[k, d + BAND].astype(f32)).astype(bf16),
                    wt[d + BAND].reshape(ncol * side, ncol * side),
                    preferred_element_type=f32)
                for d in distances
            ])

        total = 0.0
        for distances in (near, middling, far):
            await_slots(xin, fz_recv, k, distances)
            total = total + product(distances)
        return to_rows(total)

    def solve_split(values, blocks, axis):
        return jnp.concatenate(
            [
                jnp.dot(values[o * unit:(o + 1) * unit].astype(bf16), blocks[o],
                        preferred_element_type=f32)
                for o in range(ncol)
            ],
            axis=axis,
        ).astype(bf16)

    def forward_split(k):
        @pl.when(l == split_from)
        def _():
            add_parts(k)

        @pl.when(l > split_from)
        def _():
            update[...] = whole_product(k)

        solved = solve_split(stacked(sides_use, k) - update[...], inv_t, 0)
        ysol[k] = solved
        send_forward(k)
        put(ystage, k, solved.astype(f32))
        put(ysplit, k, solved.astype(f32))

    def backward_parts(k, wide):
        for distances in (far, middling, sorted(near, key=lambda d: -abs(d))):
            for d in distances:
                zout[k, d + BAND] = to_rows(jnp.dot(
                    wide, tiles_of(d + BAND), preferred_element_type=f32)).astype(bf16)
            for d in distances:
                @pl.when(exists(d))
                def _():
                    backward_copy(k, d).start()

    def backward_step(k):
        def add(total, distances):
            return functools.reduce(
                jnp.add, [zin[k, d + BAND].astype(f32) for d in distances], total)

        total = jnp.zeros_like(update)
        for distances in ([*near, *middling], far):
            await_slots(zin, bz_recv, k, distances)
            total = add(total, distances)
        wide = solve_split(stacked(ysplit, k) - total, inv, 1)

        @pl.when(l > 0)
        def _():
            backward_parts(k, wide)

        put(xstage, k, to_rows(wide.astype(f32)))

    def guest_step(k, carry):
        solved = solve_split(stacked(sides_guest, k) - whole_product(k), inv_t_guest, 0)
        put(ysplit_guest, k, solved.astype(f32))
        wide = solve_split(solved.astype(f32), inv_guest, 1)
        backward_parts(k, wide)
        put(xstage_guest, k, to_rows(wide.astype(f32)))
        return carry

    def sent(copy_of):
        def one(k, carry):
            for d in range(-BAND, BAND + 1):
                @pl.when(exists(d))
                def _():
                    copy_of(k, d).wait_send()
            return carry
        lax.fori_loop(0, chunks, one, 0)

    def middle():
        @pl.when(l < last)
        def _():
            yblock[...] = ystage[...].astype(bf16)

        @pl.when(l == last)
        def _():
            arrived(yblock, ship_recv.at[4])

        turn_start(yblock, yturned, y_send, y_recv)

        @pl.when((l == 1) | (l == 2))
        def _():
            pl.semaphore_wait(go_sem, 1)

        @pl.when((l == 1) | (l == 2) | (l == 4))
        def _():
            spread_start()
            spread_pass_on()
            spread_end()

        @pl.when(l == 3)
        def _():
            go(2)
            spread_end()

        @pl.when(l < last)
        def _():
            sent(forward_copy)

        @pl.when((l > 0) & (l < whole_from))
        def _():
            def one(k, carry):
                for o in others:
                    part_copy(k, o).wait_send()
                return carry
            lax.fori_loop(0, chunks, one, 0)

        turn_arrived(yturned, y_recv)
        turn_sent(yblock, yturned, y_send, y_recv)

        @pl.when(l < split_from)
        def _():
            for o in others:
                arrived(inv.at[o], d_recv.at[o])
            ysplit[...] = yturned[...].astype(f32)
            forward_ref[...] = yblock[...].reshape(width, side)

        @pl.when(l >= split_from)
        def _():
            forward_ref[...] = yturned[...].reshape(width, side)

    def guest():
        arrived(wb.at[:, c], ship_recv.at[0])
        spread_start()
        transpose_tiles(c)
        spread_pass_on()
        spread_end()
        go(1)
        arrived(sides_guest, ship_recv.at[1])
        arrived(inv_guest, ship_recv.at[2])
        arrived(inv_t_guest, ship_recv.at[3])
        lax.fori_loop(0, chunks, guest_step, 0)
        yblock_guest[...] = ysplit_guest[...].astype(bf16)
        ship_back_y().start()
        xblock_guest[...] = xstage_guest[...].astype(bf16)
        ship_back_x().start()
        sent(backward_copy)
        ship_back_y().wait_send()
        ship_back_x().wait_send()

    for o in others:
        inverse_copy(o).start()

    @pl.when(l < split_from)
    def _():
        sides_use[...] = sides_row[...]

    @pl.when(l >= split_from)
    def _():
        turn_start(sides_row, sides_use, s_send, s_recv)
        turn_arrived(sides_use, s_recv)
        for o in others:
            arrived(inv.at[o], d_recv.at[o])
            inv_t[o] = inv[o].T
        turn_sent(sides_row, sides_use, s_send, s_recv)

    @pl.when(l == last)
    def _():
        for copy in ship_out():
            copy.start()

    @pl.when((l == 3) | ((l >= 5) & (l < last)))
    def _():
        spread_start()
        spread_pass_on()

    @pl.when((l >= 5) & (l < last))
    def _():
        spread_end()

    @pl.when(l < last)
    def _():
        def step(t, carry):
            def stage(k, wanted, work):
                @pl.when((k >= 0) & (k < chunks) & wanted)
                def _():
                    work(k)

            stage(t, (l > 0) & (l < whole_from), forward_parts)
            stage(t - 1, l < split_from, forward_row)
            stage(t - 1, l >= split_from, forward_split)
            return carry

        lax.fori_loop(0, chunks + 1, step, 0)

    middle()

    @pl.when(l == 0)
    def _():
        guest()

    @pl.when(l < last)
    def _():
        lax.fori_loop(0, chunks, lambda k, x: (backward_step(k), x)[1], 0)
        xblock[...] = xstage[...].astype(bf16)

    @pl.when(l == last)
    def _():
        arrived(xblock, ship_recv.at[5])

    turn_start(xblock, xturned, x_send, x_recv)
    for o in others:
        inverse_copy(o).wait_send()

    @pl.when((l > 0) & (l < last))
    def _():
        sent(backward_copy)

    @pl.when(l < last)
    def _():
        for copy in (*bulk_own(), *bulk_passed()):
            copy.wait_send()

    @pl.when(l == last)
    def _():
        for copy in ship_out():
            copy.wait_send()

    turn_arrived(xturned, x_recv)
    answer_ref[...] = xturned[...].reshape(width, side)
    turn_sent(xblock, xturned, x_send, x_recv)


def upright(forward_ref, answer_ref, forward_out, answer_out):
    forward_out[...] = forward_ref[...].T
    answer_out[...] = answer_ref[...].T


def local(factor_tiles, tile_mask, inverse_diagonal, right_sides):
    nlev, nrow, ncol = (lax.axis_size(n) for n in ("level", "row", "col"))
    tiles = factor_tiles[0, :, :, 0]
    mask = tile_mask[0, :, :, 0]
    inverse = inverse_diagonal[0, 0, 0]
    sides = right_sides[0, 0, 0]
    side, width = sides.shape
    chunks = 4
    rows = width // chunks
    bf16, f32 = jnp.bfloat16, jnp.float32
    vmem = pl.BlockSpec(memory_space=pltpu.VMEM)
    hbm = pl.BlockSpec(memory_space=pltpu.HBM)
    dma = pltpu.SemaphoreType.DMA
    blocks = (ncol, rows, side)
    forward, answer = pl.pallas_call(
        functools.partial(kernel, nlev, nrow, ncol, chunks, nlev - 3),
        name="levels",
        out_shape=[jax.ShapeDtypeStruct((width, side), bf16)] * 2,
        in_specs=[hbm] * 4,
        out_specs=[vmem, vmem],
        scratch_shapes=[
            pltpu.VMEM(tiles.shape, bf16),
            pltpu.SMEM(mask.shape, mask.dtype),
            pltpu.VMEM(inverse.shape, bf16),
            pltpu.VMEM(sides.shape, f32),
            pltpu.VMEM((SLOTS, ncol, side, ncol * side), bf16),
            pltpu.VMEM((SLOTS, ncol, ncol * side, side), bf16),
            pltpu.VMEM((ncol, side, side), bf16),
            pltpu.VMEM((ncol, side, side), bf16),
            pltpu.VMEM(blocks, f32),
            pltpu.VMEM(blocks, f32),
            pltpu.VMEM((chunks, SLOTS, rows, side), bf16),
            pltpu.VMEM((chunks, *blocks), bf16),
            pltpu.VMEM((chunks, *blocks), f32),
            pltpu.VMEM((chunks, *blocks), bf16),
            pltpu.VMEM((chunks, rows, side), bf16),
            pltpu.VMEM((chunks, SLOTS, rows, side), bf16),
            pltpu.VMEM((chunks, SLOTS, rows, side), bf16),
            pltpu.VMEM((rows, side), f32),
            pltpu.VMEM(blocks, f32),
            pltpu.VMEM(blocks, f32),
            pltpu.VMEM(blocks, bf16),
            pltpu.VMEM(blocks, bf16),
            pltpu.VMEM(blocks, f32),
            pltpu.VMEM(blocks, bf16),
            pltpu.VMEM(blocks, bf16),
            dma((4,)),
            dma((chunks, SLOTS)), dma((chunks, SLOTS)),
            dma((chunks, ncol)), dma((chunks, ncol)),
            dma((chunks, SLOTS)), dma((chunks, SLOTS)),
            dma((6,)), dma((6,)),
            *[dma((ncol,)) for _ in range(8)],
            pltpu.VMEM(blocks, f32),
            pltpu.VMEM((ncol, side, side), bf16),
            pltpu.VMEM((ncol, side, side), bf16),
            pltpu.VMEM(blocks, f32),
            pltpu.VMEM(blocks, f32),
            pltpu.VMEM(blocks, bf16),
            pltpu.VMEM(blocks, bf16),
            dma((6,)), dma((6,)),
            pltpu.SemaphoreType.REGULAR,
        ],
        compiler_params=pltpu.CompilerParams(
            collective_id=0, has_side_effects=True, vmem_limit_bytes=60 * 2**20),
        cost_estimate=pl.CostEstimate(flops=2**30, bytes_accessed=2**22, transcendentals=0),
    )(tiles, mask, inverse, sides)
    forward, answer = pl.pallas_call(
        upright,
        name="upright",
        out_shape=[jax.ShapeDtypeStruct((side, width), bf16)] * 2,
        in_specs=[vmem, vmem],
        out_specs=[vmem, vmem],
    )(forward, answer)
    return (forward[None, None, None], answer[None, None, None])


def solution(mesh):
    placed = (
        P("level", "row", None, "col", None, None),
        P("level", "row", None, "col"),
        P("level", "row", "col", None, None),
        P("level", "row", "col", None, None),
    )
    return jax.shard_map(
        local,
        mesh=mesh,
        in_specs=placed,
        out_specs=(P("level", "row", "col", None, None), P("level", "row", "col", None, None)),
        check_vma=False,
    )
```

```python
import functools

import jax
import jax.numpy as jnp
from jax import lax
from jax.experimental import pallas as pl
from jax.experimental.pallas import tpu as pltpu
from jax.sharding import PartitionSpec as P

MESH = pl.DeviceIdType.MESH
BAND = 8
SLOTS = 2 * BAND + 1
HALF = BAND + 1
FAR_FIRST = sorted(range(-BAND, BAND + 1), key=lambda d: -abs(d))


def kernel(
    nlev, nrow, ncol, chunks, whole_from,
    tiles_hbm, mask_hbm, inverse_hbm, sides_hbm,
    forward_ref, answer_ref,
    tiles_ref, mask_ref, inverse_ref, sides_ref,
    wt, wb, inv, inv_t, sides_row, sides_use,
    xin, part, part_f, yin, ysol, zout, zin, update,
    ystage, ysplit, yblock, yturned, xstage, xblock, xturned,
    load_sem, fz_send, fz_recv, fy_send, fy_recv, bz_send, bz_recv,
    bulk_send, bulk_recv, d_send, d_recv, s_send, s_recv, y_send, y_recv, x_send, x_recv,
    home_wb, home_sides, yfinal, xfinal, yhome, xhome,
    ship_send, ship_recv, go_sem, near_total,
):
    p, z, c = lax.axis_index("level"), lax.axis_index("row"), lax.axis_index("col")

    def place(level):
        return jnp.where(level == 7, 5, jnp.where(level == 5, 3, jnp.where(level == 3, 7, level)))

    l = jnp.where(p == 5, 7, jnp.where(p == 3, 5, jnp.where(p == 7, 3, p)))
    moved = l != p
    side, width = sides_ref.shape
    rows = width // chunks
    unit = rows // ncol
    last = nlev - 1
    bf16, f32 = jnp.bfloat16, jnp.float32
    others = [lax.rem(c + o, ncol) for o in range(1, ncol)]
    after, before = others[0], others[-1]
    split_from = whole_from - 1
    up, down = place(l + 1), place(l - 1)

    loads = [
        pltpu.make_async_copy(src, dst, load_sem.at[n])
        for n, (src, dst) in enumerate((
            (sides_hbm, sides_ref), (inverse_hbm, inverse_ref),
            (mask_hbm, mask_ref), (tiles_hbm, tiles_ref)))
    ]
    for load in loads:
        load.start()

    def exists(d):
        return (z + d >= 0) & (z + d < nrow)

    for d in range(-BAND, BAND + 1):
        @pl.when(jnp.logical_not(exists(d)))
        def _():
            for k in range(chunks):
                xin[k, d + BAND] = jnp.zeros_like(xin[k, d + BAND])
                zin[k, d + BAND] = jnp.zeros_like(zin[k, d + BAND])

    barrier = pltpu.get_barrier_semaphore()
    for o in others:
        pl.semaphore_signal(barrier, inc=1, device_id=(p, z, o), device_id_type=MESH)

    @pl.when(l < last)
    def _():
        for q in range(nrow):
            pl.semaphore_signal(barrier, inc=1, device_id=(up, q, c), device_id_type=MESH)

    @pl.when(l > 0)
    def _():
        for q in range(nrow):
            pl.semaphore_signal(barrier, inc=1, device_id=(down, q, c), device_id_type=MESH)

    @pl.when(moved)
    def _():
        pl.semaphore_signal(barrier, inc=1, device_id=(place(p), z, c), device_id_type=MESH)
        pl.semaphore_signal(barrier, inc=1, device_id=(l, z, c), device_id_type=MESH)

    @pl.when(p == 2)
    def _():
        pl.semaphore_signal(barrier, inc=1, device_id=(3, z, c), device_id_type=MESH)

    @pl.when(p == 3)
    def _():
        pl.semaphore_signal(barrier, inc=1, device_id=(2, z, c), device_id_type=MESH)

    loads[0].wait()
    turned = sides_ref[...].T
    for o in range(ncol):
        home_sides[o] = turned[o * rows:(o + 1) * rows]
    loads[1].wait()

    @pl.when(jnp.logical_not(moved))
    def _():
        sides_row[...] = home_sides[...]
        inv[c] = inverse_ref[...]

    update[...] = jnp.zeros_like(update)
    loads[2].wait()
    loads[3].wait()

    @pl.when(p > 0)
    def _():
        def prepare(slot, carry):
            q = z + slot - BAND

            @pl.when((q >= 0) & (q < nrow))
            def _():
                for a in range(ncol):
                    present = mask_ref[a, q].astype(f32)
                    home_wb[slot, a * side:(a + 1) * side, :] = (
                        tiles_ref[a, q] * present.astype(bf16))

            @pl.when((q < 0) | (q >= nrow))
            def _():
                home_wb[slot] = jnp.zeros((ncol * side, side), bf16)

            @pl.when(jnp.logical_not(moved))
            def _():
                wb[slot, c] = home_wb[slot]
                for a in range(ncol):
                    at = slice(a * side, (a + 1) * side)
                    wt[slot, c, :, at] = home_wb[slot, at, :].T
            return carry
        lax.fori_loop(0, SLOTS, prepare, 0)

    pl.semaphore_wait(
        barrier,
        (ncol - 1)
        + jnp.where(l < last, nrow, 0)
        + jnp.where(l > 0, nrow, 0)
        + jnp.where(moved, 2, 0)
        + jnp.where((p == 2) | (p == 3), 1, 0),
    )

    def remote(src, dst, send, recv, device):
        return pltpu.make_async_remote_copy(
            src, dst, send, recv, device_id=device, device_id_type=MESH)

    def arrived(dst, sem):
        pltpu.make_async_copy(dst, dst, sem).wait()

    def forward_copy(k, d):
        return remote(
            ysol.at[k], xin.at[k, BAND - d], fz_send.at[k, BAND + d], fz_recv.at[k, BAND - d],
            (up, z + d, c))

    def backward_copy(k, d):
        return remote(
            zout.at[k, BAND + d], zin.at[k, BAND - d], bz_send.at[k, BAND + d],
            bz_recv.at[k, BAND - d], (down, z + d, c))

    def part_copy(k, o):
        return remote(
            part.at[k, o], yin.at[k, c], fy_send.at[k, o], fy_recv.at[k, c], (p, z, o))

    def turn_copy(src, dst, send, recv, o):
        return remote(src.at[o], dst.at[c], send.at[o], recv.at[c], (p, z, o))

    def turn_start(src, dst, send, recv):
        for o in others:
            turn_copy(src, dst, send, recv, o).start()
        dst[c] = src[c]

    def turn_arrived(dst, recv):
        for o in others:
            arrived(dst.at[o], recv.at[o])

    def turn_sent(src, dst, send, recv):
        for o in others:
            turn_copy(src, dst, send, recv, o).wait_send()

    def inverse_copy(o):
        return remote(inv.at[c], inv.at[c], d_send.at[o], d_recv.at[c], (p, z, o))

    low, high = pl.ds(0, HALF), pl.ds(HALF, SLOTS - HALF)

    def bulk_copy(slots, owner, n, device):
        return remote(
            wb.at[slots, owner], wb.at[slots, owner], bulk_send.at[n], bulk_recv.at[n],
            (p, z, device))

    def bulk_own():
        return [
            bulk_copy(low, c, 0, after), bulk_copy(high, c, 3, before),
            bulk_copy(high, c, 1, after), bulk_copy(low, c, 2, before),
        ]

    def bulk_passed():
        return [bulk_copy(low, before, 4, after), bulk_copy(high, after, 5, before)]

    opposite = others[1]

    def transpose_slab(owner):
        def one(slot, carry):
            for a in range(ncol):
                at = slice(a * side, (a + 1) * side)
                wt[slot, owner, :, at] = wb[slot, owner, at, :].T
            return carry
        lax.fori_loop(0, SLOTS, one, 0)

    def transpose_tiles(owner):
        @pl.when(l >= whole_from)
        def _():
            transpose_slab(owner)

    def spread_start():
        for copy in bulk_own():
            copy.start()

    def spread_pass_on():
        to_after, to_before = bulk_passed()
        arrived(wb.at[low, before], bulk_recv.at[0])
        to_after.start()
        arrived(wb.at[high, after], bulk_recv.at[3])
        to_before.start()
        arrived(wb.at[high, before], bulk_recv.at[1])
        arrived(wb.at[low, after], bulk_recv.at[2])

    def spread_end():
        transpose_tiles(before)
        transpose_tiles(after)
        arrived(wb.at[low, opposite], bulk_recv.at[4])
        arrived(wb.at[high, opposite], bulk_recv.at[5])
        transpose_tiles(opposite)

    def ship(n, src, dst, device):
        return remote(src, dst, ship_send.at[n], ship_recv.at[n], (device, z, c))

    def ship_out():
        return [
            ship(1, home_sides, sides_row, place(p)), ship(2, inverse_ref, inv.at[c], place(p)),
            ship(0, home_wb, wb.at[:, c], place(p)),
        ]

    def ship_back():
        return [ship(3, yfinal, yhome, l), ship(4, xfinal, xhome, l)]

    def go(device):
        pl.semaphore_signal(go_sem, inc=1, device_id=(device, z, c), device_id_type=MESH)

    def await_slot(buffer, sems, k, d):
        @pl.when(exists(d))
        def _():
            arrived(buffer.at[k, d + BAND], sems.at[k, d + BAND])

    def stacked(block, k):
        at = pl.ds(pl.multiple_of(k * unit, unit), unit)
        return jnp.concatenate([block[o, at] for o in range(ncol)], axis=0)

    def put(block, k, values):
        at = pl.ds(pl.multiple_of(k * unit, unit), unit)
        for o in range(ncol):
            block[o, at] = values[o * unit:(o + 1) * unit]

    def to_lanes(values):
        return jnp.concatenate([values[o * unit:(o + 1) * unit] for o in range(ncol)], axis=1)

    def to_rows(values):
        return jnp.concatenate([values[:, o * side:(o + 1) * side] for o in range(ncol)], axis=0)

    def tiles_of(slot):
        return jnp.concatenate([wb[slot, o] for o in range(ncol)], axis=1)

    def send_forward(k):
        @pl.when(l < last)
        def _():
            for d in FAR_FIRST:
                @pl.when(exists(d))
                def _():
                    forward_copy(k, d).start()

    near = range(-BAND + 3, BAND - 2)
    middling = [-BAND + 2, BAND - 2, -BAND + 1, BAND - 1]
    far = [-BAND, BAND]

    def await_slots(buffer, sems, k, distances):
        for d in sorted(distances, key=abs):
            await_slot(buffer, sems, k, d)

    def forward_product(k, distances):
        await_slots(xin, fz_recv, k, distances)
        wide = jnp.concatenate([xin[k, d + BAND] for d in distances], axis=1)
        weights = jnp.concatenate([wt[d + BAND, c] for d in distances], axis=0)
        return jnp.dot(wide, weights, preferred_element_type=f32)

    def forward_near(k):
        near_total[...] = forward_product(k, near)

    def forward_parts(k):
        total = near_total[...]
        for distances in (middling, far):
            total = total + forward_product(k, distances)

        @pl.when(l < split_from)
        def _():
            for o in range(ncol):
                part_f[k, o] = total[:, o * side:(o + 1) * side]

        @pl.when(l == split_from)
        def _():
            for o in range(ncol):
                part_f[k, o] = to_rows(total[o * unit:(o + 1) * unit])

        for o in range(ncol):
            part[k, o] = part_f[k, o].astype(bf16)
        for o in others:
            part_copy(k, o).start()

    def add_parts(k):
        mine = part_f[k, c]
        for o in others:
            arrived(yin.at[k, o], fy_recv.at[k, o])
            mine = mine + yin[k, o].astype(f32)
        update[...] = mine

    def forward_row(k):
        @pl.when(l > 0)
        def _():
            add_parts(k)

        values = (stacked(sides_use, k) - update[...]).astype(bf16)
        solved = jnp.dot(values, inv_t[c], preferred_element_type=f32).astype(bf16)
        ysol[k] = solved
        send_forward(k)
        put(ystage, k, solved.astype(f32))

    def whole_product(k):
        def product(distances):
            return functools.reduce(jnp.add, [
                jnp.dot(
                    to_lanes(xin[k, d + BAND].astype(f32)).astype(bf16),
                    wt[d + BAND].reshape(ncol * side, ncol * side),
                    preferred_element_type=f32)
                for d in distances
            ])

        total = 0.0
        for distances in (near, middling, far):
            await_slots(xin, fz_recv, k, distances)
            total = total + product(distances)
        return to_rows(total)

    def solve_split(values, blocks, axis):
        return jnp.concatenate(
            [
                jnp.dot(values[o * unit:(o + 1) * unit].astype(bf16), blocks[o],
                        preferred_element_type=f32)
                for o in range(ncol)
            ],
            axis=axis,
        ).astype(bf16)

    def forward_split(k):
        @pl.when(l == split_from)
        def _():
            add_parts(k)

        @pl.when(l > split_from)
        def _():
            update[...] = whole_product(k)

        solved = solve_split(stacked(sides_use, k) - update[...], inv_t, 0)
        ysol[k] = solved
        send_forward(k)
        put(ystage, k, solved.astype(f32))
        put(ysplit, k, solved.astype(f32))

    def backward_parts(k, wide):
        for distances in (far, middling, sorted(near, key=lambda d: -abs(d))):
            for d in distances:
                zout[k, d + BAND] = to_rows(jnp.dot(
                    wide, tiles_of(d + BAND), preferred_element_type=f32)).astype(bf16)
            for d in distances:
                @pl.when(exists(d))
                def _():
                    backward_copy(k, d).start()

    def backward_step(k):
        def add(total, distances):
            return functools.reduce(
                jnp.add, [zin[k, d + BAND].astype(f32) for d in distances], total)

        total = jnp.zeros_like(update)
        for distances in ([*near, *middling], far):
            await_slots(zin, bz_recv, k, distances)
            total = add(total, distances)
        wide = solve_split(stacked(ysplit, k) - total, inv, 1)

        @pl.when(l > 0)
        def _():
            backward_parts(k, wide)

        put(xstage, k, to_rows(wide.astype(f32)))

    def turn_round(k):
        wide = solve_split(stacked(ysplit, k), inv, 1)
        backward_parts(k, wide)
        put(xstage, k, to_rows(wide.astype(f32)))

    def sent(copy_of):
        def one(k, carry):
            for d in range(-BAND, BAND + 1):
                @pl.when(exists(d))
                def _():
                    copy_of(k, d).wait_send()
            return carry
        lax.fori_loop(0, chunks, one, 0)

    def middle():
        yblock[...] = ystage[...].astype(bf16)
        turn_start(yblock, yturned, y_send, y_recv)

        @pl.when(l == 5)
        def _():
            spread_pass_on()
            spread_end()
            go(2)

        @pl.when(l == 2)
        def _():
            go(3)
            pl.semaphore_wait(go_sem, 1)

        @pl.when((l > 0) & (l < 5))
        def _():
            spread_start()
            spread_pass_on()
            spread_end()

        @pl.when(l < last)
        def _():
            sent(forward_copy)

        @pl.when((l > 0) & (l < whole_from))
        def _():
            def one(k, carry):
                for o in others:
                    part_copy(k, o).wait_send()
                return carry
            lax.fori_loop(0, chunks, one, 0)

        turn_arrived(yturned, y_recv)
        turn_sent(yblock, yturned, y_send, y_recv)

        @pl.when(l < split_from)
        def _():
            for o in others:
                arrived(inv.at[o], d_recv.at[o])
            ysplit[...] = yturned[...].astype(f32)
            yfinal[...] = yblock[...].reshape(width, side)

        @pl.when(l >= split_from)
        def _():
            yfinal[...] = yturned[...].reshape(width, side)

    @pl.when(moved)
    def _():
        for copy in ship_out():
            copy.start()
        arrived(sides_row, ship_recv.at[1])
        arrived(inv.at[c], ship_recv.at[2])

    inv_t[c] = inv[c].T
    for o in others:
        inverse_copy(o).start()

    @pl.when(l < split_from)
    def _():
        sides_use[...] = sides_row[...]

    @pl.when(l >= split_from)
    def _():
        turn_start(sides_row, sides_use, s_send, s_recv)
        turn_arrived(sides_use, s_recv)
        for o in others:
            arrived(inv.at[o], d_recv.at[o])
            inv_t[o] = inv[o].T
        turn_sent(sides_row, sides_use, s_send, s_recv)

    @pl.when(moved)
    def _():
        arrived(wb.at[:, c], ship_recv.at[0])

    @pl.when(l == 5)
    def _():
        pl.semaphore_wait(go_sem, 1)

    @pl.when(l >= 5)
    def _():
        spread_start()

    @pl.when(moved)
    def _():
        transpose_slab(c)

    @pl.when(l > 5)
    def _():
        spread_pass_on()
        spread_end()

    def step(t, carry):
        def stage(k, wanted, work):
            @pl.when((k >= 0) & (k < chunks) & wanted)
            def _():
                work(k)

        by_parts = (l > 0) & (l < whole_from)
        stage(t, by_parts, forward_near)
        stage(t - 1, l < split_from, forward_row)
        stage(t - 1, l >= split_from, forward_split)
        stage(t - 1, l == last, turn_round)
        stage(t, by_parts, forward_parts)
        return carry

    lax.fori_loop(0, chunks + 1, step, 0)

    middle()

    @pl.when(l < last)
    def _():
        lax.fori_loop(0, chunks, lambda k, x: (backward_step(k), x)[1], 0)

    xblock[...] = xstage[...].astype(bf16)
    turn_start(xblock, xturned, x_send, x_recv)
    for o in others:
        inverse_copy(o).wait_send()

    @pl.when(l > 0)
    def _():
        sent(backward_copy)
        for copy in (*bulk_own(), *bulk_passed()):
            copy.wait_send()

    turn_arrived(xturned, x_recv)
    xfinal[...] = xturned[...].reshape(width, side)
    turn_sent(xblock, xturned, x_send, x_recv)

    @pl.when(moved)
    def _():
        for copy in ship_back():
            copy.start()
        for copy in (*ship_out(), *ship_back()):
            copy.wait_send()
        arrived(yhome, ship_recv.at[3])
        arrived(xhome, ship_recv.at[4])
        forward_ref[...] = yhome[...]
        answer_ref[...] = xhome[...]

    @pl.when(jnp.logical_not(moved))
    def _():
        forward_ref[...] = yfinal[...]
        answer_ref[...] = xfinal[...]


def upright(forward_ref, answer_ref, forward_out, answer_out):
    forward_out[...] = forward_ref[...].T
    answer_out[...] = answer_ref[...].T


def local(factor_tiles, tile_mask, inverse_diagonal, right_sides):
    nlev, nrow, ncol = (lax.axis_size(n) for n in ("level", "row", "col"))
    tiles = factor_tiles[0, :, :, 0]
    mask = tile_mask[0, :, :, 0]
    inverse = inverse_diagonal[0, 0, 0]
    sides = right_sides[0, 0, 0]
    side, width = sides.shape
    chunks = 4
    rows = width // chunks
    bf16, f32 = jnp.bfloat16, jnp.float32
    vmem = pl.BlockSpec(memory_space=pltpu.VMEM)
    hbm = pl.BlockSpec(memory_space=pltpu.HBM)
    dma = pltpu.SemaphoreType.DMA
    blocks = (ncol, rows, side)
    forward, answer = pl.pallas_call(
        functools.partial(kernel, nlev, nrow, ncol, chunks, nlev - 2),
        name="levels",
        out_shape=[jax.ShapeDtypeStruct((width, side), bf16)] * 2,
        in_specs=[hbm] * 4,
        out_specs=[vmem, vmem],
        scratch_shapes=[
            pltpu.VMEM(tiles.shape, bf16),
            pltpu.SMEM(mask.shape, mask.dtype),
            pltpu.VMEM(inverse.shape, bf16),
            pltpu.VMEM(sides.shape, f32),
            pltpu.VMEM((SLOTS, ncol, side, ncol * side), bf16),
            pltpu.VMEM((SLOTS, ncol, ncol * side, side), bf16),
            pltpu.VMEM((ncol, side, side), bf16),
            pltpu.VMEM((ncol, side, side), bf16),
            pltpu.VMEM(blocks, f32),
            pltpu.VMEM(blocks, f32),
            pltpu.VMEM((chunks, SLOTS, rows, side), bf16),
            pltpu.VMEM((chunks, *blocks), bf16),
            pltpu.VMEM((chunks, *blocks), f32),
            pltpu.VMEM((chunks, *blocks), bf16),
            pltpu.VMEM((chunks, rows, side), bf16),
            pltpu.VMEM((chunks, SLOTS, rows, side), bf16),
            pltpu.VMEM((chunks, SLOTS, rows, side), bf16),
            pltpu.VMEM((rows, side), f32),
            pltpu.VMEM(blocks, f32),
            pltpu.VMEM(blocks, f32),
            pltpu.VMEM(blocks, bf16),
            pltpu.VMEM(blocks, bf16),
            pltpu.VMEM(blocks, f32),
            pltpu.VMEM(blocks, bf16),
            pltpu.VMEM(blocks, bf16),
            dma((4,)),
            dma((chunks, SLOTS)), dma((chunks, SLOTS)),
            dma((chunks, ncol)), dma((chunks, ncol)),
            dma((chunks, SLOTS)), dma((chunks, SLOTS)),
            dma((6,)), dma((6,)),
            *[dma((ncol,)) for _ in range(8)],
            pltpu.VMEM((SLOTS, ncol * side, side), bf16),
            pltpu.VMEM(blocks, f32),
            *[pltpu.VMEM((width, side), bf16) for _ in range(4)],
            dma((5,)), dma((5,)),
            pltpu.SemaphoreType.REGULAR,
            pltpu.VMEM((rows, ncol * side), f32),
        ],
        compiler_params=pltpu.CompilerParams(
            collective_id=0, has_side_effects=True, vmem_limit_bytes=60 * 2**20),
        cost_estimate=pl.CostEstimate(flops=2**30, bytes_accessed=2**22, transcendentals=0),
    )(tiles, mask, inverse, sides)
    forward, answer = pl.pallas_call(
        upright,
        name="upright",
        out_shape=[jax.ShapeDtypeStruct((side, width), bf16)] * 2,
        in_specs=[vmem, vmem],
        out_specs=[vmem, vmem],
    )(forward, answer)
    return (forward[None, None, None], answer[None, None, None])


def solution(mesh):
    placed = (
        P("level", "row", None, "col", None, None),
        P("level", "row", None, "col"),
        P("level", "row", "col", None, None),
        P("level", "row", "col", None, None),
    )
    return jax.shard_map(
        local,
        mesh=mesh,
        in_specs=placed,
        out_specs=(P("level", "row", "col", None, None), P("level", "row", "col", None, None)),
        check_vma=False,
    )
```
